128 devices in a mesh: gx: 32 (over x, z, core), gy: 4 (over y).
Axes of the slice: x: 4, y: 4, z: 4, core: 2. Of those that a mesh axis runs over, the one named last changes fastest.
Arguments:
- field: float32 [3, 8, 2048, 2048], P(None, None, 'gx', 'gy'), may hold values from -6 to 6
Outputs:
- spectrum: float32 [2, 3, 8, 2048, 2048], P(None, None, None, ('gx', 'gy'))
The draws below stay inside these ranges and needn't reach their ends.
All inputs are finite; a program needn't handle non-finite values.
Results may differ from the reference program's by a relative error of at most 0.000092.
Values sent between devices are 32-bit elements; how exact they have to be, the bound alone decides.
A program may use at most 128 MiB of HBM per device.

```python
import jax
import jax.numpy as jnp
import numpy as np
from jax import lax

COMP = 3
PLANES = 8
NX = 2048
NY = 2048
N_GX = 32


def levels(key, shape, split, smallest, high):
    gain, own = 1.0, jax.random.fold_in(key, 6)
    for position, shards_of in split:
        draws = jnp.exp(jax.random.uniform(jax.random.fold_in(own, position), (shards_of,), jnp.float32, smallest / len(split), high / len(split)))
        gain = gain * jnp.repeat(draws, shape[position] // shards_of).reshape([-1 if axis == position else 1 for axis in range(len(shape))])
    return gain


def noise(key, dims, spread, most, split=(), kind=jnp.bfloat16):
    drawn = jax.random.normal(key, dims, jnp.float32) * spread
    if len(split) > 0:
        drawn = levels(key, dims, split, -0.22, 0.18) * drawn
    return jnp.clip(drawn, min=-most, max=most).astype(kind)


def setup_inputs(seed: int = 0) -> dict:
    keys = jax.random.split(jax.random.key(seed), 2)
    return {
        "field": noise(keys[0], (COMP, PLANES, NX, NY), 1.0, 6.0, ((2, 32), (3, 4)), jnp.float32),
    }


def frequency_order():
    digits = N_GX.bit_length() - 1
    cells = NX // N_GX
    order = np.zeros(NX, dtype=np.int32)
    for upper in range(N_GX):
        flipped = 0
        for place in range(digits):
            flipped = flipped + ((upper >> place & 1) << digits - 1 - place)
        for lower in range(cells):
            order[upper * cells + lower] = flipped + N_GX * lower
    return order

def reference(field):
    order = jnp.asarray(frequency_order()).astype(jnp.int32)
    scale = 1.0 / float(np.sqrt(NX * NY))

    def one_plane(plane):
        spec = jnp.fft.fft2(plane, axes=(1, 2)) * scale
        spec = spec[:, order, :]
        return jnp.stack([jnp.real(spec), jnp.imag(spec)]).astype(jnp.float32)
    planes = jnp.transpose(field, (1, 0, 2, 3))
    result = lax.map(one_plane, planes)
    return jnp.transpose(result, (1, 2, 0, 3, 4))
```

```python
import functools
import math

import jax
import jax.numpy as jnp
import ml_dtypes
import numpy as np
from jax import lax
from jax.experimental import pallas as pl
from jax.experimental.pallas import tpu as pltpu
from jax.sharding import PartitionSpec as P

MESH = pl.DeviceIdType.MESH
F32 = jnp.float32
BF16 = jnp.bfloat16
LANES = 128
SUB = 8
CHUNKS = 8
LAG_B = 2
LAG_C = 4


def bit_reverse(value, digits):
    return int(format(value, "0%db" % digits)[::-1], 2)


def cadd(a, b):
    im = a[1] if b[1] is None else b[1] if a[1] is None else a[1] + b[1]
    return (a[0] + b[0], im)


def csub(a, b):
    im = a[1] if b[1] is None else -b[1] if a[1] is None else a[1] - b[1]
    return (a[0] - b[0], im)


def conj(a):
    return (a[0], None if a[1] is None else -a[1])


def turn(a, k, n):
    k = k % n
    re, im = a
    if k == 0:
        return a
    if 4 * k == n:
        return (jnp.zeros_like(re) if im is None else im, -re)
    if 8 * k == n:
        h = math.sqrt(0.5)
        if im is None:
            return (re * h, re * -h)
        return ((re + im) * h, (im - re) * h)
    if 8 * k == 3 * n:
        h = math.sqrt(0.5)
        if im is None:
            return (re * -h, re * -h)
        return ((im - re) * h, (re + im) * -h)
    c, s = math.cos(2 * math.pi * k / n), -math.sin(2 * math.pi * k / n)
    if im is None:
        return (re * c, re * s)
    return (re * c - im * s, re * s + im * c)


def real_fft(values):
    n = len(values)
    if n == 1:
        return [(values[0], None)]
    if n == 2:
        return [(values[0] + values[1], None), (values[0] - values[1], None)]
    even, odd = real_fft(values[0::2]), real_fft(values[1::2])
    out = [None] * (n // 2 + 1)
    for k in range(n // 4 + 1):
        t = turn(odd[k], k, n)
        if 4 * k == n:
            out[k] = (even[k][0], -odd[k][0])
            continue
        out[k] = cadd(even[k], t)
        out[n // 2 - k] = conj(csub(even[k], t))
    return out


def complex_fft(values):
    n = len(values)
    if n == 1:
        return values
    even, odd = complex_fft(values[0::2]), complex_fft(values[1::2])
    out = [None] * n
    for k in range(n // 2):
        t = turn(odd[k], k, n)
        out[k] = cadd(even[k], t)
        out[k + n // 2] = csub(even[k], t)
    return out


def split(value):
    high = value.astype(BF16)
    return high, (value - high.astype(F32)).astype(BF16)


def split_table(table):
    high = table.astype(np.float32).astype(ml_dtypes.bfloat16)
    low = (table - high.astype(np.float64)).astype(ml_dtypes.bfloat16)
    return high, low


def root(phase, n):
    angle = -2.0 * np.pi * (phase % n) / n
    return np.cos(angle), np.sin(angle)


def tables(gx, gy, rows, cols, freqs):
    nx, ny = gx * rows, gy * cols
    groups = ny // LANES
    share = cols // groups
    per = LANES // share
    cell = np.arange(cols)
    a, e = cell // groups, cell % groups
    perm = np.zeros((gy, cols, cols), np.float32)
    for s in range(gy):
        place = e // per * LANES + (e % per + s) % per * share + a
        perm[s, cell, place] = 1.0
    tiles = rows // SUB
    m = np.arange(rows).reshape(tiles, 1, SUB)
    r = np.array([bit_reverse(i, gx.bit_length() - 1) for i in range(gx)]).reshape(1, gx, 1)
    turn_x = np.stack(root(m * r, nx), axis=2)
    turn_x = np.broadcast_to(turn_x[..., None], turn_x.shape + (LANES,))
    c, s = root(np.outer(np.arange(rows), np.arange(rows)), rows)
    dft_x = np.block([[c, -s], [s, c]])
    xh, xl = split_table(dft_x)
    x_first = np.concatenate([xh, xh], axis=1)
    dft_y = []
    lane = np.arange(LANES)
    for q in range(per):
        spot = (lane // share - q) % per * share + lane % share
        c, s = root(np.outer(spot, lane), LANES)
        dft_y.append(np.block([[c, s], [-s, c]]))
    dft_y = np.stack(dft_y) / math.sqrt(nx * ny)
    yh, yl = split_table(dft_y)
    turn_y = np.stack(root(np.outer(np.arange(groups), lane), ny), axis=1)
    turn_y = np.broadcast_to(turn_y[:, :, None, :], (groups, 2, SUB, LANES))
    return (
        perm.astype(ml_dtypes.bfloat16),
        np.ascontiguousarray(turn_x, np.float32),
        x_first,
        xl,
        yh,
        yl,
        np.ascontiguousarray(turn_y, np.float32),
    )


def kernel(
    gx, gy, planes, chunks,
    field, perm_hbm, turnx_hbm, xfirst_hbm, xlow_hbm, yhigh_hbm, ylow_hbm, turny_hbm,
    out,
    raw, s1, r1, s2, r2, s3, r3, zed, stage, perm, turnx, xfirst, xlow, yhigh, ylow, turny,
    in_sem, tab_sem, ss1, rs1, ss2, rs2, ss3, rs3, out_sem,
):
    me, my = lax.axis_index("gx"), lax.axis_index("gy")
    step = planes // chunks
    rows, cols = raw.shape[1:]
    tiles, wide = rows // SUB, cols // LANES
    freqs = r3.shape[3]
    groups = turny.shape[0]
    per = yhigh.shape[0]

    def part(c):
        return pl.ds(c * step, step)

    def load(c):
        return pltpu.make_async_copy(field.at[part(c)], raw.at[part(c)], in_sem.at[c])

    loads = [
        pltpu.make_async_copy(a, b, tab_sem.at[i])
        for i, (a, b) in enumerate(
            [
                (perm_hbm.at[my], perm),
                (turnx_hbm.at[me // wide], turnx),
                (xfirst_hbm, xfirst),
                (xlow_hbm, xlow),
                (yhigh_hbm, yhigh),
                (ylow_hbm, ylow),
                (turny_hbm, turny),
            ]
        )
    ]

    barrier = pltpu.get_barrier_semaphore()

    def greet(i, _):
        pl.semaphore_signal(barrier, inc=1, device_id=(lax.rem(me + i, gx), my), device_id_type=MESH)
        return 0

    lax.fori_loop(1, gx, greet, 0)
    for j in range(1, gy):
        pl.semaphore_signal(barrier, inc=1, device_id=(me, lax.rem(my + j, gy)), device_id_type=MESH)
    loads[0].start()
    lax.fori_loop(0, chunks, lambda c, _: (load(c).start(), 0)[1], 0)
    for copy in loads[1:]:
        copy.start()
    pl.semaphore_wait(barrier, gx + gy - 2)
    loads[0].wait()

    def exchange_x(c, source, target, send, recv):
        pltpu.make_async_copy(source.at[me, part(c)], target.at[me, part(c)], recv.at[c]).start()

        def one(i, _):
            t = lax.rem(me + i, gx)
            pltpu.make_async_remote_copy(
                src_ref=source.at[t, part(c)],
                dst_ref=target.at[me, part(c)],
                send_sem=send.at[c],
                recv_sem=recv.at[c],
                device_id=(t, my),
                device_id_type=MESH,
            ).start()
            return 0

        lax.fori_loop(1, gx, one, 0)

    def exchange_y(c):
        pltpu.make_async_copy(s3.at[my, part(c)], r3.at[my, part(c)], rs3.at[c]).start()
        for j in range(1, gy):
            t = lax.rem(my + j, gy)
            pltpu.make_async_remote_copy(
                src_ref=s3.at[t, part(c)],
                dst_ref=r3.at[my, part(c)],
                send_sem=ss3.at[c],
                recv_sem=rs3.at[c],
                device_id=(me, t),
                device_id_type=MESH,
            ).start()

    def arrived(c, target, recv):
        pltpu.make_async_copy(target.at[:, part(c)], target.at[:, part(c)], recv.at[c]).wait()

    def sent(c, source, send):
        some = source.at[pl.ds(1, source.shape[0] - 1), part(c)]
        pltpu.make_async_copy(some, some, send.at[c]).wait()

    def permute(c):
        load(c).wait()

        def one(p, _):
            plane = c * step + p
            high, low = split(raw[plane])
            both = jnp.dot(jnp.concatenate([high, low], axis=0), perm[...], preferred_element_type=F32)
            moved = both[:rows] + both[rows:]
            for t in range(tiles):
                for w in range(wide):
                    s1[t * wide + w, plane] = moved[t * SUB : (t + 1) * SUB, w * LANES : (w + 1) * LANES]
            return 0

        lax.fori_loop(0, step, one, 0)

    def over_gx(c):
        def one(p, _):
            plane = c * step + p
            got = real_fft([r1[g, plane] for g in range(gx)])
            for i in range(gx):
                r = bit_reverse(i, gx.bit_length() - 1)
                re, im = got[r] if 2 * r <= gx else conj(got[gx - r])
                if r == 0:
                    s2[i, plane, 0] = re
                    s2[i, plane, 1] = jnp.zeros_like(re)
                    continue
                tr, ti = turnx[i, 0], turnx[i, 1]
                if im is None:
                    s2[i, plane, 0] = re * tr
                    s2[i, plane, 1] = re * ti
                else:
                    s2[i, plane, 0] = re * tr - im * ti
                    s2[i, plane, 1] = re * ti + im * tr
            return 0

        lax.fori_loop(0, step, one, 0)

    def over_m(c):
        def one(p, _):
            plane = c * step + p
            value = jnp.concatenate(
                [
                    jnp.concatenate(
                        [r2[t * wide + w, plane, part_] for part_ in range(2) for t in range(tiles)], axis=0
                    )
                    for w in range(wide)
                ],
                axis=1,
            )
            high, low = split(value)
            done = jnp.dot(xfirst[...], jnp.concatenate([high, low], axis=0), preferred_element_type=F32)
            done = done + jnp.dot(xlow[...], high, preferred_element_type=F32)
            for part_ in range(2):
                for s in range(gy):
                    first = part_ * rows + s * freqs
                    s3[s, plane, part_] = done[first : first + freqs]
            return 0

        lax.fori_loop(0, step, one, 0)

    def result(c):
        slot = lax.rem(c, 2)
        return pltpu.make_async_copy(stage.at[slot], out.at[:, part(c)], out_sem.at[slot])

    def over_y(c):
        slot = lax.rem(c, 2)
        group = lax.broadcasted_iota(jnp.int32, (freqs, LANES), 1) // (LANES // per)

        def one(p, _):
            plane = c * step + p
            for q in range(per):
                lines = []
                for w in range(wide):
                    halves = []
                    for part_ in range(2):
                        got = [r3[s, plane, part_, :, w * LANES : (w + 1) * LANES] for s in range(gy)]
                        merged = got[-q % per]
                        for g in range(1, per):
                            merged = jnp.where(group == g, got[(g - q) % per], merged)
                        halves.append(merged)
                    lines.append(jnp.concatenate(halves, axis=1))
                high, low = split(jnp.concatenate(lines, axis=0))
                both = jnp.dot(jnp.concatenate([high, low], axis=0), yhigh[q], preferred_element_type=F32)
                total = wide * freqs
                done = both[:total] + both[total:] + jnp.dot(high, ylow[q], preferred_element_type=F32)
                for w in range(wide):
                    zed[w * per + q] = done[w * freqs : (w + 1) * freqs]
            for b in range(freqs // SUB):
                at = slice(b * SUB, (b + 1) * SUB)
                values = []
                for e in range(groups):
                    re, im = zed[e, at, :LANES], zed[e, at, LANES:]
                    if e == 0:
                        values.append((re, im))
                    else:
                        tr, ti = turny[e, 0], turny[e, 1]
                        values.append((re * tr - im * ti, re * ti + im * tr))
                for k, (re, im) in enumerate(complex_fft(values)):
                    stage[slot, 0, p, at, k * LANES : (k + 1) * LANES] = re
                    stage[slot, 1, p, at, k * LANES : (k + 1) * LANES] = im
            return 0

        lax.fori_loop(0, step, one, 0)

    def enter(c, _):
        permute(c)
        exchange_x(c, s1, r1, ss1, rs1)
        return 0

    lax.fori_loop(0, chunks, enter, 0)
    for copy in loads[1:]:
        copy.wait()

    def turn_step(i, _):
        @pl.when(i < chunks)
        def _():
            arrived(i, r1, rs1)
            over_gx(i)
            exchange_x(i, s2, r2, ss2, rs2)

        @pl.when(jnp.logical_and(i >= LAG_B, i < chunks + LAG_B))
        def _():
            c = i - LAG_B
            arrived(c, r2, rs2)
            over_m(c)
            exchange_y(c)

        @pl.when(i >= LAG_C)
        def _():
            c = i - LAG_C
            arrived(c, r3, rs3)

            @pl.when(c >= 2)
            def _():
                result(c - 2).wait()

            over_y(c)
            result(c).start()

        return 0

    lax.fori_loop(0, chunks + LAG_C, turn_step, 0)

    def finish(c, _):
        sent(c, s1, ss1)
        sent(c, s2, ss2)
        sent(c, s3, ss3)
        return 0

    lax.fori_loop(0, chunks, finish, 0)
    for c in (chunks - 2, chunks - 1):
        result(c).wait()


def solution(mesh):
    gx, gy = mesh.shape["gx"], mesh.shape["gy"]

    def per_device(field):
        comp, depth, rows, cols = field.shape
        planes = comp * depth
        freqs = rows // gy
        ny = gy * cols
        groups = ny // LANES
        step = planes // CHUNKS
        consts = tables(gx, gy, rows, cols, freqs)
        any_ = pl.BlockSpec(memory_space=pl.ANY)
        pieces = (rows // SUB) * (cols // LANES)
        assert pieces == gx
        vmem = lambda a: pltpu.VMEM(a.shape, a.dtype)
        dma = pltpu.SemaphoreType.DMA
        perm, turnx, xfirst, xlow, yhigh, ylow, turny = consts
        result = pl.pallas_call(
            functools.partial(kernel, gx, gy, planes, CHUNKS),
            out_shape=jax.ShapeDtypeStruct((2, planes, freqs, ny), F32),
            in_specs=[any_] * 8,
            out_specs=any_,
            scratch_shapes=[
                pltpu.VMEM((planes, rows, cols), F32),
                pltpu.VMEM((gx, planes, SUB, LANES), F32),
                pltpu.VMEM((gx, planes, SUB, LANES), F32),
                pltpu.VMEM((gx, planes, 2, SUB, LANES), F32),
                pltpu.VMEM((gx, planes, 2, SUB, LANES), F32),
                pltpu.VMEM((gy, planes, 2, freqs, cols), F32),
                pltpu.VMEM((gy, planes, 2, freqs, cols), F32),
                pltpu.VMEM((groups, freqs, 2 * LANES), F32),
                pltpu.VMEM((2, 2, step, freqs, ny), F32),
                pltpu.VMEM(perm.shape[1:], perm.dtype),
                pltpu.VMEM(turnx.shape[1:], turnx.dtype),
                vmem(xfirst),
                vmem(xlow),
                vmem(yhigh),
                vmem(ylow),
                vmem(turny),
                dma((CHUNKS,)),
                dma((7,)),
                dma((CHUNKS,)),
                dma((CHUNKS,)),
                dma((CHUNKS,)),
                dma((CHUNKS,)),
                dma((CHUNKS,)),
                dma((CHUNKS,)),
                dma((2,)),
            ],
            compiler_params=pltpu.CompilerParams(
                collective_id=0, has_side_effects=True, vmem_limit_bytes=56 << 20
            ),
        )(field.reshape(planes, rows, cols), *[jnp.asarray(c) for c in consts])
        return result.reshape(2, comp, depth, freqs, ny)

    return jax.shard_map(
        per_device,
        mesh=mesh,
        in_specs=(P(None, None, "gx", "gy"),),
        out_specs=P(None, None, None, ("gx", "gy"), None),
        check_vma=False,
    )
```

```python
import functools
import math

import jax
import jax.numpy as jnp
import ml_dtypes
import numpy as np
from jax import lax
from jax.experimental import pallas as pl
from jax.experimental.pallas import tpu as pltpu
from jax.sharding import PartitionSpec as P

MESH = pl.DeviceIdType.MESH
F32 = jnp.float32
BF16 = jnp.bfloat16
LANES = 128
SUB = 8
CHUNKS = 24
LAG_B = 2
LAG_C = 4


def bit_reverse(value, digits):
    return int(format(value, "0%db" % digits)[::-1], 2)


def cadd(a, b):
    im = a[1] if b[1] is None else b[1] if a[1] is None else a[1] + b[1]
    return (a[0] + b[0], im)


def csub(a, b):
    im = a[1] if b[1] is None else -b[1] if a[1] is None else a[1] - b[1]
    return (a[0] - b[0], im)


def conj(a):
    return (a[0], None if a[1] is None else -a[1])


def turn(a, k, n):
    k = k % n
    re, im = a
    if k == 0:
        return a
    if 4 * k == n:
        return (jnp.zeros_like(re) if im is None else im, -re)
    if 8 * k == n:
        h = math.sqrt(0.5)
        if im is None:
            return (re * h, re * -h)
        return ((re + im) * h, (im - re) * h)
    if 8 * k == 3 * n:
        h = math.sqrt(0.5)
        if im is None:
            return (re * -h, re * -h)
        return ((im - re) * h, (re + im) * -h)
    c, s = math.cos(2 * math.pi * k / n), -math.sin(2 * math.pi * k / n)
    if im is None:
        return (re * c, re * s)
    return (re * c - im * s, re * s + im * c)


def real_fft(values):
    n = len(values)
    if n == 1:
        return [(values[0], None)]
    if n == 2:
        return [(values[0] + values[1], None), (values[0] - values[1], None)]
    even, odd = real_fft(values[0::2]), real_fft(values[1::2])
    out = [None] * (n // 2 + 1)
    for k in range(n // 4 + 1):
        t = turn(odd[k], k, n)
        if 4 * k == n:
            out[k] = (even[k][0], -odd[k][0])
            continue
        out[k] = cadd(even[k], t)
        out[n // 2 - k] = conj(csub(even[k], t))
    return out


def complex_fft(values):
    n = len(values)
    if n == 1:
        return values
    even, odd = complex_fft(values[0::2]), complex_fft(values[1::2])
    out = [None] * n
    for k in range(n // 2):
        t = turn(odd[k], k, n)
        out[k] = cadd(even[k], t)
        out[k + n // 2] = csub(even[k], t)
    return out


def split(value):
    high = value.astype(BF16)
    return high, (value - high.astype(F32)).astype(BF16)


def split_table(table):
    high = table.astype(np.float32).astype(ml_dtypes.bfloat16)
    low = (table - high.astype(np.float64)).astype(ml_dtypes.bfloat16)
    return high, low


def root(phase, n):
    angle = -2.0 * np.pi * (phase % n) / n
    return np.cos(angle), np.sin(angle)


def tables(gx, gy, rows, cols, freqs):
    nx, ny = gx * rows, gy * cols
    groups = ny // LANES
    share = cols // groups
    per = LANES // share
    cell = np.arange(cols)
    a, e = cell // groups, cell % groups
    perm = np.zeros((gy, cols, cols), np.float32)
    for s in range(gy):
        place = e // per * LANES + (e % per + s) % per * share + a
        perm[s, cell, place] = 1.0
    tiles = rows // SUB
    m = np.arange(rows).reshape(tiles, 1, SUB)
    r = np.array([bit_reverse(i, gx.bit_length() - 1) for i in range(gx)]).reshape(1, gx, 1)
    turn_x = np.stack(root(m * r, nx), axis=2)
    turn_x = np.broadcast_to(turn_x[..., None], turn_x.shape + (LANES,))
    c, s = root(np.outer(np.arange(rows), np.arange(rows)), rows)
    dft_x = np.block([[c, -s], [s, c]])
    xh, xl = split_table(dft_x)
    x_first = np.concatenate([xh, xh], axis=1)
    dft_y = []
    lane = np.arange(LANES)
    for q in range(per):
        spot = (lane // share - q) % per * share + lane % share
        c, s = root(np.outer(spot, lane), LANES)
        dft_y.append(np.block([[c, s], [-s, c]]))
    dft_y = np.stack(dft_y) / math.sqrt(nx * ny)
    yh, yl = split_table(dft_y)
    turn_y = np.stack(root(np.outer(np.arange(groups), lane), ny), axis=1)
    turn_y = np.broadcast_to(turn_y[:, :, None, :], (groups, 2, SUB, LANES))
    return (
        perm.astype(ml_dtypes.bfloat16),
        np.ascontiguousarray(turn_x, np.float32),
        x_first,
        xl,
        yh,
        yl,
        np.ascontiguousarray(turn_y, np.float32),
    )


def kernel(
    gx, gy, planes, chunks,
    field, perm_hbm, turnx_hbm, xfirst_hbm, xlow_hbm, yhigh_hbm, ylow_hbm, turny_hbm,
    out,
    raw, s1, r1, s2, r2, s3, r3, zed, stage, perm, turnx, xfirst, xlow, yhigh, ylow, turny,
    in_sem, tab_sem, ss1, rs1, ss2, rs2, ss3, rs3, out_sem,
):
    me, my = lax.axis_index("gx"), lax.axis_index("gy")
    step = planes // chunks
    rows, cols = raw.shape[1:]
    tiles, wide = rows // SUB, cols // LANES
    freqs = r3.shape[3]
    groups = turny.shape[0]
    per = yhigh.shape[0]

    def part(c):
        return pl.ds(c * step, step)

    def load(c):
        return pltpu.make_async_copy(field.at[part(c)], raw.at[part(c)], in_sem.at[c])

    loads = [
        pltpu.make_async_copy(a, b, tab_sem.at[i])
        for i, (a, b) in enumerate(
            [
                (perm_hbm.at[my], perm),
                (turnx_hbm.at[me // wide], turnx),
                (xfirst_hbm, xfirst),
                (xlow_hbm, xlow),
                (yhigh_hbm, yhigh),
                (ylow_hbm, ylow),
                (turny_hbm, turny),
            ]
        )
    ]

    barrier = pltpu.get_barrier_semaphore()

    def greet(i, _):
        pl.semaphore_signal(barrier, inc=1, device_id=(lax.rem(me + i, gx), my), device_id_type=MESH)
        return 0

    lax.fori_loop(1, gx, greet, 0)
    for j in range(1, gy):
        pl.semaphore_signal(barrier, inc=1, device_id=(me, lax.rem(my + j, gy)), device_id_type=MESH)
    loads[0].start()
    lax.fori_loop(0, chunks, lambda c, _: (load(c).start(), 0)[1], 0)
    for copy in loads[1:]:
        copy.start()
    pl.semaphore_wait(barrier, gx + gy - 2)
    loads[0].wait()

    def exchange_x(c, source, target, send, recv):
        pltpu.make_async_copy(source.at[me, part(c)], target.at[me, part(c)], recv.at[c]).start()

        def one(i, _):
            t = lax.rem(me + i, gx)
            pltpu.make_async_remote_copy(
                src_ref=source.at[t, part(c)],
                dst_ref=target.at[me, part(c)],
                send_sem=send.at[c],
                recv_sem=recv.at[c],
                device_id=(t, my),
                device_id_type=MESH,
            ).start()
            return 0

        lax.fori_loop(1, gx, one, 0)

    def exchange_y(c):
        pltpu.make_async_copy(s3.at[my, part(c)], r3.at[my, part(c)], rs3.at[c]).start()
        for j in range(1, gy):
            t = lax.rem(my + j, gy)
            pltpu.make_async_remote_copy(
                src_ref=s3.at[t, part(c)],
                dst_ref=r3.at[my, part(c)],
                send_sem=ss3.at[c],
                recv_sem=rs3.at[c],
                device_id=(me, t),
                device_id_type=MESH,
            ).start()

    def arrived(c, target, recv):
        pltpu.make_async_copy(target.at[:, part(c)], target.at[:, part(c)], recv.at[c]).wait()

    def sent(c, source, send):
        some = source.at[pl.ds(1, source.shape[0] - 1), part(c)]
        pltpu.make_async_copy(some, some, send.at[c]).wait()

    def permute(c):
        load(c).wait()

        def one(p, _):
            plane = c * step + p
            high, low = split(raw[plane])
            both = jnp.dot(jnp.concatenate([high, low], axis=0), perm[...], preferred_element_type=F32)
            moved = both[:rows] + both[rows:]
            for t in range(tiles):
                for w in range(wide):
                    s1[t * wide + w, plane] = moved[t * SUB : (t + 1) * SUB, w * LANES : (w + 1) * LANES]
            return 0

        lax.fori_loop(0, step, one, 0)

    def over_gx(c):
        def one(p, _):
            plane = c * step + p
            got = real_fft([r1[g, plane] for g in range(gx)])
            for i in range(gx):
                r = bit_reverse(i, gx.bit_length() - 1)
                re, im = got[r] if 2 * r <= gx else conj(got[gx - r])
                if r == 0:
                    s2[i, plane, 0] = re
                    s2[i, plane, 1] = jnp.zeros_like(re)
                    continue
                tr, ti = turnx[i, 0], turnx[i, 1]
                if im is None:
                    s2[i, plane, 0] = re * tr
                    s2[i, plane, 1] = re * ti
                else:
                    s2[i, plane, 0] = re * tr - im * ti
                    s2[i, plane, 1] = re * ti + im * tr
            return 0

        lax.fori_loop(0, step, one, 0)

    def over_m(c):
        def one(p, _):
            plane = c * step + p
            value = jnp.concatenate(
                [
                    jnp.concatenate(
                        [r2[t * wide + w, plane, part_] for part_ in range(2) for t in range(tiles)], axis=0
                    )
                    for w in range(wide)
                ],
                axis=1,
            )
            high, low = split(value)
            done = jnp.dot(xfirst[...], jnp.concatenate([high, low], axis=0), preferred_element_type=F32)
            done = done + jnp.dot(xlow[...], high, preferred_element_type=F32)
            for part_ in range(2):
                for s in range(gy):
                    first = part_ * rows + s * freqs
                    s3[s, plane, part_] = done[first : first + freqs]
            return 0

        lax.fori_loop(0, step, one, 0)

    def result(c):
        slot = lax.rem(c, 2)
        return pltpu.make_async_copy(stage.at[slot], out.at[:, part(c)], out_sem.at[slot])

    def over_y(c):
        slot = lax.rem(c, 2)
        group = lax.broadcasted_iota(jnp.int32, (freqs, LANES), 1) // (LANES // per)

        def one(p, _):
            plane = c * step + p
            for q in range(per):
                lines = []
                for w in range(wide):
                    halves = []
                    for part_ in range(2):
                        got = [r3[s, plane, part_, :, w * LANES : (w + 1) * LANES] for s in range(gy)]
                        merged = got[-q % per]
                        for g in range(1, per):
                            merged = jnp.where(group == g, got[(g - q) % per], merged)
                        halves.append(merged)
                    lines.append(jnp.concatenate(halves, axis=1))
                high, low = split(jnp.concatenate(lines, axis=0))
                both = jnp.dot(jnp.concatenate([high, low], axis=0), yhigh[q], preferred_element_type=F32)
                total = wide * freqs
                done = both[:total] + both[total:] + jnp.dot(high, ylow[q], preferred_element_type=F32)
                for w in range(wide):
                    zed[w * per + q] = done[w * freqs : (w + 1) * freqs]
            for b in range(freqs // SUB):
                at = slice(b * SUB, (b + 1) * SUB)
                values = []
                for e in range(groups):
                    re, im = zed[e, at, :LANES], zed[e, at, LANES:]
                    if e == 0:
                        values.append((re, im))
                    else:
                        tr, ti = turny[e, 0], turny[e, 1]
                        values.append((re * tr - im * ti, re * ti + im * tr))
                for k, (re, im) in enumerate(complex_fft(values)):
                    stage[slot, 0, p, at, k * LANES : (k + 1) * LANES] = re
                    stage[slot, 1, p, at, k * LANES : (k + 1) * LANES] = im
            return 0

        lax.fori_loop(0, step, one, 0)

    def enter(c, _):
        permute(c)
        exchange_x(c, s1, r1, ss1, rs1)
        return 0

    lax.fori_loop(0, chunks, enter, 0)
    for copy in loads[1:]:
        copy.wait()

    def turn_step(i, _):
        @pl.when(i < chunks)
        def _():
            arrived(i, r1, rs1)
            over_gx(i)
            exchange_x(i, s2, r2, ss2, rs2)

        @pl.when(jnp.logical_and(i >= LAG_B, i < chunks + LAG_B))
        def _():
            c = i - LAG_B
            arrived(c, r2, rs2)
            over_m(c)
            exchange_y(c)

        @pl.when(i >= LAG_C)
        def _():
            c = i - LAG_C
            arrived(c, r3, rs3)

            @pl.when(c >= 2)
            def _():
                result(c - 2).wait()

            over_y(c)
            result(c).start()

        return 0

    lax.fori_loop(0, chunks + LAG_C, turn_step, 0)

    def finish(c, _):
        sent(c, s1, ss1)
        sent(c, s2, ss2)
        sent(c, s3, ss3)
        return 0

    lax.fori_loop(0, chunks, finish, 0)
    for c in (chunks - 2, chunks - 1):
        result(c).wait()


def solution(mesh):
    gx, gy = mesh.shape["gx"], mesh.shape["gy"]

    def per_device(field):
        comp, depth, rows, cols = field.shape
        planes = comp * depth
        freqs = rows // gy
        ny = gy * cols
        groups = ny // LANES
        step = planes // CHUNKS
        consts = tables(gx, gy, rows, cols, freqs)
        any_ = pl.BlockSpec(memory_space=pl.ANY)
        pieces = (rows // SUB) * (cols // LANES)
        assert pieces == gx
        vmem = lambda a: pltpu.VMEM(a.shape, a.dtype)
        dma = pltpu.SemaphoreType.DMA
        perm, turnx, xfirst, xlow, yhigh, ylow, turny = consts
        result = pl.pallas_call(
            functools.partial(kernel, gx, gy, planes, CHUNKS),
            out_shape=jax.ShapeDtypeStruct((2, planes, freqs, ny), F32),
            in_specs=[any_] * 8,
            out_specs=any_,
            scratch_shapes=[
                pltpu.VMEM((planes, rows, cols), F32),
                pltpu.VMEM((gx, planes, SUB, LANES), F32),
                pltpu.VMEM((gx, planes, SUB, LANES), F32),
                pltpu.VMEM((gx, planes, 2, SUB, LANES), F32),
                pltpu.VMEM((gx, planes, 2, SUB, LANES), F32),
                pltpu.VMEM((gy, planes, 2, freqs, cols), F32),
                pltpu.VMEM((gy, planes, 2, freqs, cols), F32),
                pltpu.VMEM((groups, freqs, 2 * LANES), F32),
                pltpu.VMEM((2, 2, step, freqs, ny), F32),
                pltpu.VMEM(perm.shape[1:], perm.dtype),
                pltpu.VMEM(turnx.shape[1:], turnx.dtype),
                vmem(xfirst),
                vmem(xlow),
                vmem(yhigh),
                vmem(ylow),
                vmem(turny),
                dma((CHUNKS,)),
                dma((7,)),
                dma((CHUNKS,)),
                dma((CHUNKS,)),
                dma((CHUNKS,)),
                dma((CHUNKS,)),
                dma((CHUNKS,)),
                dma((CHUNKS,)),
                dma((2,)),
            ],
            compiler_params=pltpu.CompilerParams(
                collective_id=0, has_side_effects=True, vmem_limit_bytes=56 << 20
            ),
        )(field.reshape(planes, rows, cols), *[jnp.asarray(c) for c in consts])
        return result.reshape(2, comp, depth, freqs, ny)

    return jax.shard_map(
        per_device,
        mesh=mesh,
        in_specs=(P(None, None, "gx", "gy"),),
        out_specs=P(None, None, None, ("gx", "gy"), None),
        check_vma=False,
    )
```

```python
import functools
import math

import jax
import jax.numpy as jnp
import ml_dtypes
import numpy as np
from jax import lax
from jax.experimental import pallas as pl
from jax.experimental.pallas import tpu as pltpu
from jax.sharding import PartitionSpec as P

MESH = pl.DeviceIdType.MESH
F32 = jnp.float32
BF16 = jnp.bfloat16
LANES = 128
SUB = 8
WRITES = 8
PLACES = (2, 8, 4, 16)
FAMILIES = len(PLACES)
AHEAD = 6
LAG_A = 4
LAG_B = 7
LAG_C = 9


def bit_reverse(value, digits):
    return int(format(value, "0%db" % digits)[::-1], 2)


def cadd(a, b):
    im = a[1] if b[1] is None else b[1] if a[1] is None else a[1] + b[1]
    return (a[0] + b[0], im)


def csub(a, b):
    im = a[1] if b[1] is None else -b[1] if a[1] is None else a[1] - b[1]
    return (a[0] - b[0], im)


def conj(a):
    return (a[0], None if a[1] is None else -a[1])


def turn(a, k, n):
    k = k % n
    re, im = a
    if k == 0:
        return a
    if 4 * k == n:
        return (jnp.zeros_like(re) if im is None else im, -re)
    if 8 * k == n:
        h = math.sqrt(0.5)
        if im is None:
            return (re * h, re * -h)
        return ((re + im) * h, (im - re) * h)
    if 8 * k == 3 * n:
        h = math.sqrt(0.5)
        if im is None:
            return (re * -h, re * -h)
        return ((im - re) * h, (re + im) * -h)
    c, s = math.cos(2 * math.pi * k / n), -math.sin(2 * math.pi * k / n)
    if im is None:
        return (re * c, re * s)
    return (re * c - im * s, re * s + im * c)


def real_fft(values):
    n = len(values)
    if n == 1:
        return [(values[0], None)]
    if n == 2:
        return [(values[0] + values[1], None), (values[0] - values[1], None)]
    even, odd = real_fft(values[0::2]), real_fft(values[1::2])
    out = [None] * (n // 2 + 1)
    for k in range(n // 4 + 1):
        t = turn(odd[k], k, n)
        if 4 * k == n:
            out[k] = (even[k][0], -odd[k][0])
            continue
        out[k] = cadd(even[k], t)
        out[n // 2 - k] = conj(csub(even[k], t))
    return out


def complex_fft(values):
    n = len(values)
    if n == 1:
        return values
    even, odd = complex_fft(values[0::2]), complex_fft(values[1::2])
    out = [None] * n
    for k in range(n // 2):
        t = turn(odd[k], k, n)
        out[k] = cadd(even[k], t)
        out[k + n // 2] = csub(even[k], t)
    return out


def split(value):
    high = value.astype(BF16)
    return high, (value - high.astype(F32)).astype(BF16)


def split_table(table):
    high = table.astype(np.float32).astype(ml_dtypes.bfloat16)
    low = (table - high.astype(np.float64)).astype(ml_dtypes.bfloat16)
    return high, low


def root(phase, n):
    angle = -2.0 * np.pi * (phase % n) / n
    return np.cos(angle), np.sin(angle)


def tables(gx, gy, rows, cols, freqs):
    nx, ny = gx * rows, gy * cols
    groups = ny // LANES
    share = cols // groups
    per = LANES // share
    cell = np.arange(cols)
    a, e = cell // groups, cell % groups
    perm = np.zeros((gy, cols, cols), np.float32)
    for s in range(gy):
        place = e // per * LANES + (e % per + s) % per * share + a
        perm[s, cell, place] = 1.0
    tiles = rows // SUB
    m = np.arange(rows).reshape(tiles, 1, SUB)
    r = np.array([bit_reverse(i, gx.bit_length() - 1) for i in range(gx)]).reshape(1, gx, 1)
    turn_x = np.stack(root(m * r, nx), axis=2)
    turn_x = np.broadcast_to(turn_x[..., None], turn_x.shape + (LANES,))
    c, s = root(np.outer(np.arange(rows), np.arange(rows)), rows)
    dft_x = np.block([[c, -s], [s, c]])
    xh, xl = split_table(dft_x)
    x_first = np.concatenate([xh, xh], axis=1)
    dft_y = []
    lane = np.arange(LANES)
    for q in range(per):
        spot = (lane // share - q) % per * share + lane % share
        c, s = root(np.outer(spot, lane), LANES)
        dft_y.append(np.block([[c, s], [-s, c]]))
    dft_y = np.stack(dft_y) / math.sqrt(nx * ny)
    yh, yl = split_table(dft_y)
    turn_y = np.stack(root(np.outer(np.arange(groups), lane), ny), axis=1)
    turn_y = np.broadcast_to(turn_y[:, :, None, :], (groups, 2, SUB, LANES))
    return (
        perm.astype(ml_dtypes.bfloat16),
        np.ascontiguousarray(turn_x, np.float32),
        x_first,
        xl,
        yh,
        yl,
        np.ascontiguousarray(turn_y, np.float32),
    )


def gray(g):
    x1, x0, z1, z0, c = g // 16, g // 8 % 2, g // 4 % 2, g // 2 % 2, g % 2
    return x1 * 16 + (x1 + x0) % 2 * 8 + z1 * 4 + (z1 + z0) % 2 * 2 + c


def ungray(code):
    x1, xv, z1, zv, c = code // 16, code // 8 % 2, code // 4 % 2, code // 2 % 2, code % 2
    return x1 * 16 + (x1 + xv) % 2 * 8 + z1 * 4 + (z1 + zv) % 2 * 2 + c


def kernel(
    gx, gy, planes,
    field, perm_hbm, turnx_hbm, xfirst_hbm, xlow_hbm, yhigh_hbm, ylow_hbm, turny_hbm,
    out,
    raw, s1, r1, s2, r2, s3, r3, zed, perm, turnx, xfirst, xlow, yhigh, ylow, turny,
    in_sem, tab_sem, ss1, rs1, ssf, rsf, ss2, rs2, ss3, rs3,
):
    me, my = lax.axis_index("gx"), lax.axis_index("gy")
    code = gray(me)
    rows, cols = raw.shape[1:]
    tiles, wide = rows // SUB, cols // LANES
    freqs = r3.shape[3]
    groups = turny.shape[0]
    per = yhigh.shape[0]
    half = gx // 2

    def bit_of(family):
        place = PLACES[0]
        for f in range(1, FAMILIES):
            place = jnp.where(family == f, PLACES[f], place)
        return place, code // place % 2

    def piece(place):
        return code // (2 * place) * place + code % place

    def device(index, place, bit):
        return ungray(index // place * (2 * place) + bit * place + index % place)

    def load(c):
        return pltpu.make_async_copy(field.at[c], raw.at[c], in_sem.at[c])

    pairs = [(perm_hbm.at[my], perm)]
    for f in range(FAMILIES):
        pairs.append((turnx_hbm.at[piece(PLACES[f]) * 2 // wide], turnx.at[f]))
    pairs += [
        (xfirst_hbm, xfirst),
        (xlow_hbm, xlow),
        (yhigh_hbm, yhigh),
        (ylow_hbm, ylow),
        (turny_hbm, turny),
    ]
    loads = [pltpu.make_async_copy(a, b, tab_sem.at[i]) for i, (a, b) in enumerate(pairs)]

    barrier = pltpu.get_barrier_semaphore()

    def greet(i, _):
        pl.semaphore_signal(barrier, inc=1, device_id=(lax.rem(me + i, gx), my), device_id_type=MESH)
        return 0

    lax.fori_loop(1, gx, greet, 0)
    for j in range(1, gy):
        pl.semaphore_signal(barrier, inc=1, device_id=(me, lax.rem(my + j, gy)), device_id_type=MESH)
    loads[0].start()
    lax.fori_loop(0, planes, lambda c, _: (load(c).start(), 0)[1], 0)
    for copy in loads[1:]:
        copy.start()
    pl.semaphore_wait(barrier, gx + gy - 2)
    loads[0].wait()

    def send(source, target, send_sem, recv_sem, device_id):
        pltpu.make_async_remote_copy(
            src_ref=source,
            dst_ref=target,
            send_sem=send_sem,
            recv_sem=recv_sem,
            device_id=device_id,
            device_id_type=MESH,
        ).start()

    def wait(ref, sem):
        pltpu.make_async_copy(ref, ref, sem).wait()

    def exchange_raw(c):
        place, bit = bit_of(lax.rem(c, FAMILIES))
        own = piece(place)
        pltpu.make_async_copy(s1.at[c, pl.ds(2 * own, 2)], r1.at[c, me], rs1.at[c]).start()

        def one(k, _):
            i = lax.rem(own + k, half)
            send(s1.at[c, pl.ds(2 * i, 2)], r1.at[c, me], ss1.at[c], rs1.at[c], (device(i, place, bit), my))
            return 0

        lax.fori_loop(1, half, one, 0)

    def forward(c):
        place, bit = bit_of(lax.rem(c, FAMILIES))
        other = ungray(code + place - 2 * place * bit)

        def one(i, _):
            g = device(i, place, bit)
            send(r1.at[c, g], r1.at[c, g], ssf.at[c], rsf.at[c], (other, my))
            return 0

        lax.fori_loop(0, half, one, 0)

    def exchange_x(c):
        place, bit = bit_of(lax.rem(c, FAMILIES))
        own = piece(place)
        pltpu.make_async_copy(s2.at[c, me], r2.at[c, own], rs2.at[c]).start()

        def one(k, _):
            t = device(lax.rem(own + k, half), place, bit)
            send(s2.at[c, t], r2.at[c, own], ss2.at[c], rs2.at[c], (t, my))
            return 0

        lax.fori_loop(1, half, one, 0)

    def exchange_y(c):
        pltpu.make_async_copy(s3.at[my, c], r3.at[my, c], rs3.at[c]).start()
        for j in range(1, gy):
            t = lax.rem(my + j, gy)
            send(s3.at[t, c], r3.at[my, c], ss3.at[c], rs3.at[c], (me, t))

    def permute(c):
        load(c).wait()
        high, low = split(raw[c])
        both = jnp.dot(jnp.concatenate([high, low], axis=0), perm[...], preferred_element_type=F32)
        moved = both[:rows] + both[rows:]
        for t in range(tiles):
            for w in range(wide):
                s1[c, t * wide + w] = moved[t * SUB : (t + 1) * SUB, w * LANES : (w + 1) * LANES]

    def over_gx(c):
        family = lax.rem(c, FAMILIES)

        def one(w, _):
            got = real_fft([r1[c, g, w] for g in range(gx)])
            for i in range(gx):
                r = bit_reverse(i, gx.bit_length() - 1)
                re, im = got[r] if 2 * r <= gx else conj(got[gx - r])
                if r == 0:
                    s2[c, i, w, 0] = re
                    s2[c, i, w, 1] = jnp.zeros_like(re)
                    continue
                tr, ti = turnx[family, i, 0], turnx[family, i, 1]
                if im is None:
                    s2[c, i, w, 0] = re * tr
                    s2[c, i, w, 1] = re * ti
                else:
                    s2[c, i, w, 0] = re * tr - im * ti
                    s2[c, i, w, 1] = re * ti + im * tr
            return 0

        lax.fori_loop(0, 2, one, 0)

    def over_m(c):
        value = jnp.concatenate(
            [
                jnp.concatenate(
                    [r2[c, (t * wide + w) // 2, w % 2, part] for part in range(2) for t in range(tiles)], axis=0
                )
                for w in range(wide)
            ],
            axis=1,
        )
        high, low = split(value)
        done = jnp.dot(xfirst[...], jnp.concatenate([high, low], axis=0), preferred_element_type=F32)
        done = done + jnp.dot(xlow[...], high, preferred_element_type=F32)
        for part in range(2):
            for s in range(gy):
                first = part * rows + s * freqs
                s3[s, c, part] = done[first : first + freqs]

    def over_y(c):
        group = lax.broadcasted_iota(jnp.int32, (freqs, LANES), 1) // (LANES // per)
        for q in range(per):
            lines = []
            for w in range(wide):
                halves = []
                for part in range(2):
                    got = [r3[s, c, part, :, w * LANES : (w + 1) * LANES] for s in range(gy)]
                    merged = got[-q % per]
                    for g in range(1, per):
                        merged = jnp.where(group == g, got[(g - q) % per], merged)
                    halves.append(merged)
                lines.append(jnp.concatenate(halves, axis=1))
            high, low = split(jnp.concatenate(lines, axis=0))
            both = jnp.dot(jnp.concatenate([high, low], axis=0), yhigh[q], preferred_element_type=F32)
            total = wide * freqs
            done = both[:total] + both[total:] + jnp.dot(high, ylow[q], preferred_element_type=F32)
            for w in range(wide):
                zed[w * per + q] = done[w * freqs : (w + 1) * freqs]
        for b in range(freqs // SUB):
            at = slice(b * SUB, (b + 1) * SUB)
            values = []
            for e in range(groups):
                re, im = zed[e, at, :LANES], zed[e, at, LANES:]
                if e == 0:
                    values.append((re, im))
                else:
                    tr, ti = turny[e, 0], turny[e, 1]
                    values.append((re * tr - im * ti, re * ti + im * tr))
            for k, (re, im) in enumerate(complex_fft(values)):
                out[0, c, at, k * LANES : (k + 1) * LANES] = re
                out[1, c, at, k * LANES : (k + 1) * LANES] = im

    def enter(c, _):
        permute(c)
        exchange_raw(c)
        return 0

    lax.fori_loop(0, AHEAD, enter, 0)
    for copy in loads[1:]:
        copy.wait()

    def turn_step(i, _):
        @pl.when(i < planes - AHEAD)
        def _():
            enter(i + AHEAD, 0)

        @pl.when(i < planes)
        def _():
            wait(r1.at[i, pl.ds(0, half)], rs1.at[i])
            forward(i)

        @pl.when(jnp.logical_and(i >= LAG_A, i < planes + LAG_A))
        def _():
            c = i - LAG_A
            wait(r1.at[c, pl.ds(0, half)], rsf.at[c])
            over_gx(c)
            exchange_x(c)

        @pl.when(jnp.logical_and(i >= LAG_B, i < planes + LAG_B))
        def _():
            c = i - LAG_B
            wait(r2.at[c], rs2.at[c])
            over_m(c)
            exchange_y(c)

        @pl.when(i >= LAG_C)
        def _():
            c = i - LAG_C
            wait(r3.at[:, c], rs3.at[c])
            over_y(c)

        return 0

    lax.fori_loop(0, planes + LAG_C, turn_step, 0)

    def finish(c, _):
        wait(s1.at[c, pl.ds(0, 2 * (half - 1))], ss1.at[c])
        wait(r1.at[c, pl.ds(0, half)], ssf.at[c])
        wait(s2.at[c, pl.ds(0, half - 1)], ss2.at[c])
        wait(s3.at[pl.ds(0, gy - 1), c], ss3.at[c])
        return 0

    lax.fori_loop(0, planes, finish, 0)


def write_out(done, out, sems):
    size = done.shape[1] // (WRITES // 2)
    copies = []
    for i in range(WRITES):
        at = (i % 2, pl.ds(i // 2 * size, size))
        copies.append(pltpu.make_async_copy(done.at[at], out.at[at], sems.at[i]))
        copies[-1].start()
    for copy in copies:
        copy.wait()


def solution(mesh):
    gx, gy = mesh.shape["gx"], mesh.shape["gy"]

    def per_device(field):
        comp, depth, rows, cols = field.shape
        planes = comp * depth
        freqs = rows // gy
        ny = gy * cols
        groups = ny // LANES
        consts = tables(gx, gy, rows, cols, freqs)
        any_ = pl.BlockSpec(memory_space=pl.ANY)
        pieces = (rows // SUB) * (cols // LANES)
        assert pieces == gx
        vmem = lambda a: pltpu.VMEM(a.shape, a.dtype)
        dma = pltpu.SemaphoreType.DMA
        perm, turnx, xfirst, xlow, yhigh, ylow, turny = consts
        result = pl.pallas_call(
            functools.partial(kernel, gx, gy, planes),
            out_shape=pltpu.VMEM((2, planes, freqs, ny), F32),
            in_specs=[any_] * 8,
            out_specs=pl.BlockSpec(memory_space=pltpu.VMEM),
            scratch_shapes=[
                pltpu.VMEM((planes, rows, cols), F32),
                pltpu.VMEM((planes, gx, SUB, LANES), F32),
                pltpu.VMEM((planes, gx, 2, SUB, LANES), F32),
                pltpu.VMEM((planes, gx, 2, 2, SUB, LANES), F32),
                pltpu.VMEM((planes, gx // 2, 2, 2, SUB, LANES), F32),
                pltpu.VMEM((gy, planes, 2, freqs, cols), F32),
                pltpu.VMEM((gy, planes, 2, freqs, cols), F32),
                pltpu.VMEM((groups, freqs, 2 * LANES), F32),
                pltpu.VMEM(perm.shape[1:], perm.dtype),
                pltpu.VMEM((FAMILIES,) + turnx.shape[1:], turnx.dtype),
                vmem(xfirst),
                vmem(xlow),
                vmem(yhigh),
                vmem(ylow),
                vmem(turny),
                dma((planes,)),
                dma((6 + FAMILIES,)),
                *[dma((planes,))] * 8,
            ],
            compiler_params=pltpu.CompilerParams(
                collective_id=0, has_side_effects=True, vmem_limit_bytes=50 << 20
            ),
        )(field.reshape(planes, rows, cols), *[jnp.asarray(c) for c in consts])
        result = pltpu.with_memory_space_constraint(result, pltpu.VMEM)
        result = pl.pallas_call(
            write_out,
            out_shape=jax.ShapeDtypeStruct(result.shape, F32),
            in_specs=[pl.BlockSpec(memory_space=pltpu.VMEM)],
            out_specs=any_,
            scratch_shapes=[dma((WRITES,))],
            compiler_params=pltpu.CompilerParams(vmem_limit_bytes=8 << 20),
        )(result)
        return result.reshape(2, comp, depth, freqs, ny)

    return jax.shard_map(
        per_device,
        mesh=mesh,
        in_specs=(P(None, None, "gx", "gy"),),
        out_specs=P(None, None, None, ("gx", "gy"), None),
        check_vma=False,
    )
```

```python
import functools
import math

import jax
import jax.numpy as jnp
import ml_dtypes
import numpy as np
from jax import lax
from jax.experimental import pallas as pl
from jax.experimental.pallas import tpu as pltpu
from jax.sharding import PartitionSpec as P

MESH = pl.DeviceIdType.MESH
F32 = jnp.float32
BF16 = jnp.bfloat16
LANES = 128
SUB = 8
WRITES = 8
PLACES = (2, 8, 4, 16)
FAMILIES = len(PLACES)
AHEAD = 9
LAG_A = 6
LAG_B = 11
LAG_C = 15


def bit_reverse(value, digits):
    return int(format(value, "0%db" % digits)[::-1], 2)


def cadd(a, b):
    im = a[1] if b[1] is None else b[1] if a[1] is None else a[1] + b[1]
    return (a[0] + b[0], im)


def csub(a, b):
    im = a[1] if b[1] is None else -b[1] if a[1] is None else a[1] - b[1]
    return (a[0] - b[0], im)


def conj(a):
    return (a[0], None if a[1] is None else -a[1])


def turn(a, k, n):
    k = k % n
    re, im = a
    if k == 0:
        return a
    if 4 * k == n:
        return (jnp.zeros_like(re) if im is None else im, -re)
    if 8 * k == n:
        h = math.sqrt(0.5)
        if im is None:
            return (re * h, re * -h)
        return ((re + im) * h, (im - re) * h)
    if 8 * k == 3 * n:
        h = math.sqrt(0.5)
        if im is None:
            return (re * -h, re * -h)
        return ((im - re) * h, (re + im) * -h)
    c, s = math.cos(2 * math.pi * k / n), -math.sin(2 * math.pi * k / n)
    if im is None:
        return (re * c, re * s)
    return (re * c - im * s, re * s + im * c)


def real_fft(values):
    n = len(values)
    if n == 1:
        return [(values[0], None)]
    if n == 2:
        return [(values[0] + values[1], None), (values[0] - values[1], None)]
    even, odd = real_fft(values[0::2]), real_fft(values[1::2])
    out = [None] * (n // 2 + 1)
    for k in range(n // 4 + 1):
        t = turn(odd[k], k, n)
        if 4 * k == n:
            out[k] = (even[k][0], -odd[k][0])
            continue
        out[k] = cadd(even[k], t)
        out[n // 2 - k] = conj(csub(even[k], t))
    return out


def complex_fft(values):
    n = len(values)
    if n == 1:
        return values
    even, odd = complex_fft(values[0::2]), complex_fft(values[1::2])
    out = [None] * n
    for k in range(n // 2):
        t = turn(odd[k], k, n)
        out[k] = cadd(even[k], t)
        out[k + n // 2] = csub(even[k], t)
    return out


def split(value):
    high = value.astype(BF16)
    return high, (value - high.astype(F32)).astype(BF16)


def split_table(table):
    high = table.astype(np.float32).astype(ml_dtypes.bfloat16)
    low = (table - high.astype(np.float64)).astype(ml_dtypes.bfloat16)
    return high, low


def root(phase, n):
    angle = -2.0 * np.pi * (phase % n) / n
    return np.cos(angle), np.sin(angle)


def tables(gx, gy, rows, cols, freqs):
    nx, ny = gx * rows, gy * cols
    groups = ny // LANES
    share = cols // groups
    per = LANES // share
    cell = np.arange(cols)
    a, e = cell // groups, cell % groups
    perm = np.zeros((gy, cols, cols), np.float32)
    for s in range(gy):
        place = e // per * LANES + (e % per + s) % per * share + a
        perm[s, cell, place] = 1.0
    tiles = rows // SUB
    m = np.arange(rows).reshape(tiles, 1, SUB)
    r = np.array([bit_reverse(i, gx.bit_length() - 1) for i in range(gx)]).reshape(1, gx, 1)
    turn_x = np.stack(root(m * r, nx), axis=2)
    turn_x = np.broadcast_to(turn_x[..., None], turn_x.shape + (LANES,))
    c, s = root(np.outer(np.arange(rows), np.arange(rows)), rows)
    dft_x = np.block([[c, -s], [s, c]])
    xh, xl = split_table(dft_x)
    x_first = np.concatenate([xh, xh], axis=1)
    dft_y = []
    lane = np.arange(LANES)
    for q in range(per):
        spot = (lane // share - q) % per * share + lane % share
        c, s = root(np.outer(spot, lane), LANES)
        dft_y.append(np.block([[c, s], [-s, c]]))
    dft_y = np.stack(dft_y) / math.sqrt(nx * ny)
    yh, yl = split_table(dft_y)
    turn_y = np.stack(root(np.outer(np.arange(groups), lane), ny), axis=1)
    turn_y = np.broadcast_to(turn_y[:, :, None, :], (groups, 2, SUB, LANES))
    return (
        perm.astype(ml_dtypes.bfloat16),
        np.ascontiguousarray(turn_x, np.float32),
        x_first,
        xl,
        yh,
        yl,
        np.ascontiguousarray(turn_y, np.float32),
    )


def gray(g):
    x1, x0, z1, z0, c = g // 16, g // 8 % 2, g // 4 % 2, g // 2 % 2, g % 2
    return x1 * 16 + (x1 + x0) % 2 * 8 + z1 * 4 + (z1 + z0) % 2 * 2 + c


def ungray(code):
    x1, xv, z1, zv, c = code // 16, code // 8 % 2, code // 4 % 2, code // 2 % 2, code % 2
    return x1 * 16 + (x1 + xv) % 2 * 8 + z1 * 4 + (z1 + zv) % 2 * 2 + c


def kernel(
    gx, gy, planes,
    field, perm_hbm, turnx_hbm, xfirst_hbm, xlow_hbm, yhigh_hbm, ylow_hbm, turny_hbm,
    out,
    raw, s1, r1, s2, r2, s3, r3, zed, perm, turnx, xfirst, xlow, yhigh, ylow, turny,
    in_sem, tab_sem, ss1, rs1, ssf, rsf, ss2, rs2, ss3, rs3,
):
    me, my = lax.axis_index("gx"), lax.axis_index("gy")
    code = gray(me)
    rows, cols = raw.shape[1:]
    tiles, wide = rows // SUB, cols // LANES
    freqs = r3.shape[3]
    groups = turny.shape[0]
    per = yhigh.shape[0]
    half = gx // 2
    units = 2 * planes

    def toggles(value, weights):
        return [(1 - value // w % 2 * 2) * w for w in weights]

    flip_me = toggles(me, [1 << i for i in range(gx.bit_length() - 1)])

    def flipped(value, flips, mask):
        for i, f in enumerate(flips):
            if mask >> i & 1:
                value = value + f
        return value

    def piece(place):
        return code // (2 * place) * place + code % place

    def by_family(c, body):
        for f, place in enumerate(PLACES):

            @pl.when(lax.rem(c, FAMILIES) == f)
            def _(place=place):
                body(place)

    def peers(place):
        return [(k, ungray(k // place * (2 * place) + k % place)) for k in range(half)]

    def load(c):
        return pltpu.make_async_copy(field.at[c], raw.at[c], in_sem.at[c])

    pairs = [(perm_hbm.at[my], perm)]
    for f in range(FAMILIES):
        pairs.append((turnx_hbm.at[piece(PLACES[f]) * 2 // wide], turnx.at[f]))
    pairs += [
        (xfirst_hbm, xfirst),
        (xlow_hbm, xlow),
        (yhigh_hbm, yhigh),
        (ylow_hbm, ylow),
        (turny_hbm, turny),
    ]
    loads = [pltpu.make_async_copy(a, b, tab_sem.at[i]) for i, (a, b) in enumerate(pairs)]

    barrier = pltpu.get_barrier_semaphore()

    def greet(i, _):
        pl.semaphore_signal(barrier, inc=1, device_id=(lax.rem(me + i, gx), my), device_id_type=MESH)
        return 0

    lax.fori_loop(1, gx, greet, 0)
    for j in range(1, gy):
        pl.semaphore_signal(barrier, inc=1, device_id=(me, lax.rem(my + j, gy)), device_id_type=MESH)
    loads[0].start()
    lax.fori_loop(0, planes, lambda c, _: (load(c).start(), 0)[1], 0)
    for copy in loads[1:]:
        copy.start()
    pl.semaphore_wait(barrier, gx + gy - 2)
    loads[0].wait()

    def send(source, target, send_sem, recv_sem, device_id):
        pltpu.make_async_remote_copy(
            src_ref=source,
            dst_ref=target,
            send_sem=send_sem,
            recv_sem=recv_sem,
            device_id=device_id,
            device_id_type=MESH,
        ).start()

    def wait(ref, sem):
        pltpu.make_async_copy(ref, ref, sem).wait()

    def exchange_raw(c):
        def body(place):
            own = piece(place)
            flips = toggles(own, [1 << i for i in range(half.bit_length() - 1)])
            pltpu.make_async_copy(s1.at[c, own], r1.at[c, me], rs1.at[c]).start()
            for k, mask in peers(place)[1:]:
                there = (flipped(me, flip_me, mask), my)
                send(s1.at[c, flipped(own, flips, k)], r1.at[c, me], ss1, rs1.at[c], there)

        by_family(c, body)

    def forward(c):
        def body(place):
            other = (flipped(me, flip_me, ungray(place)), my)
            for k, mask in peers(place):
                g = flipped(me, flip_me, mask)
                send(r1.at[c, g], r1.at[c, g], ssf, rsf.at[c], other)

        by_family(c, body)

    def exchange_x(c):
        def body(place):
            own = piece(place)
            pltpu.make_async_copy(s2.at[c, me], r2.at[c, own], rs2.at[c]).start()
            for k, mask in peers(place)[1:]:
                there = flipped(me, flip_me, mask)
                send(s2.at[c, there], r2.at[c, own], ss2, rs2.at[c], (there, my))

        by_family(c, body)

    def exchange_y(c):
        pltpu.make_async_copy(s3.at[my, c], r3.at[my, c], rs3.at[c]).start()
        for j in range(1, gy):
            t = lax.rem(my + j, gy)
            send(s3.at[t, c], r3.at[my, c], ss3, rs3.at[c], (me, t))

    def permute(c):
        load(c).wait()
        high, low = split(raw[c])
        both = jnp.dot(jnp.concatenate([high, low], axis=0), perm[...], preferred_element_type=F32)
        moved = both[:rows] + both[rows:]
        for t in range(tiles):
            for w in range(wide):
                s1[2 * c + w % 2, (t * wide + w) // 2] = moved[t * SUB : (t + 1) * SUB, w * LANES : (w + 1) * LANES]

    def over_gx(c):
        family = lax.rem(c, FAMILIES)

        got = real_fft([r1[c, g] for g in range(gx)])
        for i in range(gx):
            r = bit_reverse(i, gx.bit_length() - 1)
            re, im = got[r] if 2 * r <= gx else conj(got[gx - r])
            if r == 0:
                s2[c, i, 0] = re
                s2[c, i, 1] = jnp.zeros_like(re)
                continue
            tr, ti = turnx[family, i, 0], turnx[family, i, 1]
            if im is None:
                s2[c, i, 0] = re * tr
                s2[c, i, 1] = re * ti
            else:
                s2[c, i, 0] = re * tr - im * ti
                s2[c, i, 1] = re * ti + im * tr

    def over_m(c):
        value = jnp.concatenate(
            [
                jnp.concatenate(
                    [r2[c, t * wide // 2 + w, part] for part in range(2) for t in range(tiles)], axis=0
                )
                for w in range(wide // 2)
            ],
            axis=1,
        )
        high, low = split(value)
        done = jnp.dot(xfirst[...], jnp.concatenate([high, low], axis=0), preferred_element_type=F32)
        done = done + jnp.dot(xlow[...], high, preferred_element_type=F32)
        for part in range(2):
            for s in range(gy):
                first = part * rows + s * freqs
                s3[s, c, part] = done[first : first + freqs]

    def over_y(c):
        group = lax.broadcasted_iota(jnp.int32, (freqs, LANES), 1) // (LANES // per)
        for q in range(per):
            lines = []
            for w in range(wide):
                halves = []
                for part in range(2):
                    at = slice(w // 2 * LANES, (w // 2 + 1) * LANES)
                    got = [r3[s, 2 * c + w % 2, part, :, at] for s in range(gy)]
                    merged = got[-q % per]
                    for g in range(1, per):
                        merged = jnp.where(group == g, got[(g - q) % per], merged)
                    halves.append(merged)
                lines.append(jnp.concatenate(halves, axis=1))
            high, low = split(jnp.concatenate(lines, axis=0))
            both = jnp.dot(jnp.concatenate([high, low], axis=0), yhigh[q], preferred_element_type=F32)
            total = wide * freqs
            done = both[:total] + both[total:] + jnp.dot(high, ylow[q], preferred_element_type=F32)
            for w in range(wide):
                zed[w * per + q] = done[w * freqs : (w + 1) * freqs]
        for b in range(freqs // SUB):
            at = slice(b * SUB, (b + 1) * SUB)
            values = []
            for e in range(groups):
                re, im = zed[e, at, :LANES], zed[e, at, LANES:]
                if e == 0:
                    values.append((re, im))
                else:
                    tr, ti = turny[e, 0], turny[e, 1]
                    values.append((re * tr - im * ti, re * ti + im * tr))
            for k, (re, im) in enumerate(complex_fft(values)):
                out[0, c, at, k * LANES : (k + 1) * LANES] = re
                out[1, c, at, k * LANES : (k + 1) * LANES] = im

    def enter(c, _):
        @pl.when(lax.rem(c, 2) == 0)
        def _():
            permute(lax.div(c, 2))

        exchange_raw(c)
        return 0

    lax.fori_loop(0, AHEAD, enter, 0)
    for copy in loads[1:]:
        copy.wait()

    def turn_step(i, _):
        @pl.when(i < units - AHEAD)
        def _():
            enter(i + AHEAD, 0)

        @pl.when(i < units)
        def _():
            wait(r1.at[i, pl.ds(0, half)], rs1.at[i])
            forward(i)

        @pl.when(jnp.logical_and(i >= LAG_A, i < units + LAG_A))
        def _():
            c = i - LAG_A
            wait(r1.at[c, pl.ds(0, half)], rsf.at[c])
            over_gx(c)
            exchange_x(c)

        @pl.when(jnp.logical_and(i >= LAG_B, i < units + LAG_B))
        def _():
            c = i - LAG_B
            wait(r2.at[c], rs2.at[c])
            over_m(c)
            exchange_y(c)

        @pl.when(i >= LAG_C)
        def _():
            c = i - LAG_C
            wait(r3.at[:, c], rs3.at[c])

            @pl.when(lax.rem(c, 2) == 1)
            def _():
                over_y(lax.div(c, 2))

        return 0

    lax.fori_loop(0, units + LAG_C, turn_step, 0)

    wait(s1.at[:, pl.ds(0, half - 1)], ss1)
    wait(r1.at[:, pl.ds(0, half)], ssf)
    wait(s2.at[:, pl.ds(0, half - 1)], ss2)
    wait(s3.at[pl.ds(0, gy - 1)], ss3)


def write_out(done, out, sems):
    size = done.shape[1] // (WRITES // 2)
    copies = []
    for i in range(WRITES):
        at = (i % 2, pl.ds(i // 2 * size, size))
        copies.append(pltpu.make_async_copy(done.at[at], out.at[at], sems.at[i]))
        copies[-1].start()
    for copy in copies:
        copy.wait()


def solution(mesh):
    gx, gy = mesh.shape["gx"], mesh.shape["gy"]

    def per_device(field):
        comp, depth, rows, cols = field.shape
        planes = comp * depth
        units = 2 * planes
        freqs = rows // gy
        ny = gy * cols
        groups = ny // LANES
        consts = tables(gx, gy, rows, cols, freqs)
        any_ = pl.BlockSpec(memory_space=pl.ANY)
        pieces = (rows // SUB) * (cols // LANES)
        assert pieces == gx
        vmem = lambda a: pltpu.VMEM(a.shape, a.dtype)
        dma = pltpu.SemaphoreType.DMA
        perm, turnx, xfirst, xlow, yhigh, ylow, turny = consts
        result = pl.pallas_call(
            functools.partial(kernel, gx, gy, planes),
            out_shape=pltpu.VMEM((2, planes, freqs, ny), F32),
            in_specs=[any_] * 8,
            out_specs=pl.BlockSpec(memory_space=pltpu.VMEM),
            scratch_shapes=[
                pltpu.VMEM((planes, rows, cols), F32),
                pltpu.VMEM((units, gx // 2, SUB, LANES), F32),
                pltpu.VMEM((units, gx, SUB, LANES), F32),
                pltpu.VMEM((units, gx, 2, SUB, LANES), F32),
                pltpu.VMEM((units, gx // 2, 2, SUB, LANES), F32),
                pltpu.VMEM((gy, units, 2, freqs, cols // 2), F32),
                pltpu.VMEM((gy, units, 2, freqs, cols // 2), F32),
                pltpu.VMEM((groups, freqs, 2 * LANES), F32),
                pltpu.VMEM(perm.shape[1:], perm.dtype),
                pltpu.VMEM((FAMILIES,) + turnx.shape[1:], turnx.dtype),
                vmem(xfirst),
                vmem(xlow),
                vmem(yhigh),
                vmem(ylow),
                vmem(turny),
                dma((planes,)),
                dma((6 + FAMILIES,)),
                *[pltpu.SemaphoreType.DMA, dma((units,))] * 4,
            ],
            compiler_params=pltpu.CompilerParams(
                collective_id=0, has_side_effects=True, vmem_limit_bytes=50 << 20
            ),
        )(field.reshape(planes, rows, cols), *[jnp.asarray(c) for c in consts])
        result = pltpu.with_memory_space_constraint(result, pltpu.VMEM)
        result = pl.pallas_call(
            write_out,
            out_shape=jax.ShapeDtypeStruct(result.shape, F32),
            in_specs=[pl.BlockSpec(memory_space=pltpu.VMEM)],
            out_specs=any_,
            scratch_shapes=[dma((WRITES,))],
            compiler_params=pltpu.CompilerParams(vmem_limit_bytes=8 << 20),
        )(result)
        return result.reshape(2, comp, depth, freqs, ny)

    return jax.shard_map(
        per_device,
        mesh=mesh,
        in_specs=(P(None, None, "gx", "gy"),),
        out_specs=P(None, None, None, ("gx", "gy"), None),
        check_vma=False,
    )
```

```python
import functools
import math

import jax
import jax.numpy as jnp
import ml_dtypes
import numpy as np
from jax import lax
from jax.experimental import pallas as pl
from jax.experimental.pallas import tpu as pltpu
from jax.sharding import PartitionSpec as P

MESH = pl.DeviceIdType.MESH
F32 = jnp.float32
BF16 = jnp.bfloat16
LANES = 128
SUB = 8
WRITES = 8
PLACES = (2, 8, 4, 16)
FAMILIES = len(PLACES)
AHEAD = 12
LAG_A = 8
LAG_B = 13
LAG_C = 17


def bit_reverse(value, digits):
    return int(format(value, "0%db" % digits)[::-1], 2)


def cadd(a, b):
    im = a[1] if b[1] is None else b[1] if a[1] is None else a[1] + b[1]
    return (a[0] + b[0], im)


def csub(a, b):
    im = a[1] if b[1] is None else -b[1] if a[1] is None else a[1] - b[1]
    return (a[0] - b[0], im)


def conj(a):
    return (a[0], None if a[1] is None else -a[1])


def turn(a, k, n):
    k = k % n
    re, im = a
    if k == 0:
        return a
    if 4 * k == n:
        return (jnp.zeros_like(re) if im is None else im, -re)
    if 8 * k == n:
        h = math.sqrt(0.5)
        if im is None:
            return (re * h, re * -h)
        return ((re + im) * h, (im - re) * h)
    if 8 * k == 3 * n:
        h = math.sqrt(0.5)
        if im is None:
            return (re * -h, re * -h)
        return ((im - re) * h, (re + im) * -h)
    c, s = math.cos(2 * math.pi * k / n), -math.sin(2 * math.pi * k / n)
    if im is None:
        return (re * c, re * s)
    return (re * c - im * s, re * s + im * c)


def real_fft(values):
    n = len(values)
    if n == 1:
        return [(values[0], None)]
    if n == 2:
        return [(values[0] + values[1], None), (values[0] - values[1], None)]
    even, odd = real_fft(values[0::2]), real_fft(values[1::2])
    out = [None] * (n // 2 + 1)
    for k in range(n // 4 + 1):
        t = turn(odd[k], k, n)
        if 4 * k == n:
            out[k] = (even[k][0], -odd[k][0])
            continue
        out[k] = cadd(even[k], t)
        out[n // 2 - k] = conj(csub(even[k], t))
    return out


def complex_fft(values):
    n = len(values)
    if n == 1:
        return values
    even, odd = complex_fft(values[0::2]), complex_fft(values[1::2])
    out = [None] * n
    for k in range(n // 2):
        t = turn(odd[k], k, n)
        out[k] = cadd(even[k], t)
        out[k + n // 2] = csub(even[k], t)
    return out


def split(value):
    high = value.astype(BF16)
    return high, (value - high.astype(F32)).astype(BF16)


def split_table(table):
    high = table.astype(np.float32).astype(ml_dtypes.bfloat16)
    low = (table - high.astype(np.float64)).astype(ml_dtypes.bfloat16)
    return high, low


def root(phase, n):
    angle = -2.0 * np.pi * (phase % n) / n
    return np.cos(angle), np.sin(angle)


def tables(gx, gy, rows, cols, freqs):
    nx, ny = gx * rows, gy * cols
    groups = ny // LANES
    share = cols // groups
    per = LANES // share
    cell = np.arange(cols)
    a, e = cell // groups, cell % groups
    perm = np.zeros((gy, cols, cols), np.float32)
    for s in range(gy):
        place = e // per * LANES + (e % per + s) % per * share + a
        perm[s, cell, place] = 1.0
    tiles = rows // SUB
    m = np.arange(rows).reshape(tiles, 1, SUB)
    r = np.array([bit_reverse(i, gx.bit_length() - 1) for i in range(gx)]).reshape(1, gx, 1)
    turn_x = np.stack(root(m * r, nx), axis=2)
    turn_x = np.broadcast_to(turn_x[..., None], turn_x.shape + (LANES,))
    c, s = root(np.outer(np.arange(rows), np.arange(rows)), rows)
    dft_x = np.block([[c, -s], [s, c]])
    xh, xl = split_table(dft_x)
    x_first = np.concatenate([xh, xh], axis=1)
    dft_y = []
    lane = np.arange(LANES)
    for q in range(per):
        spot = (lane // share - q) % per * share + lane % share
        c, s = root(np.outer(spot, lane), LANES)
        dft_y.append(np.block([[c, s], [-s, c]]))
    dft_y = np.stack(dft_y) / math.sqrt(nx * ny)
    yh, yl = split_table(dft_y)
    turn_y = np.stack(root(np.outer(np.arange(groups), lane), ny), axis=1)
    turn_y = np.broadcast_to(turn_y[:, :, None, :], (groups, 2, SUB, LANES))
    return (
        perm.astype(ml_dtypes.bfloat16),
        np.ascontiguousarray(turn_x, np.float32),
        x_first,
        xl,
        yh,
        yl,
        np.ascontiguousarray(turn_y, np.float32),
    )


def gray(g):
    x1, x0, z1, z0, c = g // 16, g // 8 % 2, g // 4 % 2, g // 2 % 2, g % 2
    return x1 * 16 + (x1 + x0) % 2 * 8 + z1 * 4 + (z1 + z0) % 2 * 2 + c


def ungray(code):
    x1, xv, z1, zv, c = code // 16, code // 8 % 2, code // 4 % 2, code // 2 % 2, code % 2
    return x1 * 16 + (x1 + xv) % 2 * 8 + z1 * 4 + (z1 + zv) % 2 * 2 + c


def kernel(
    gx, gy, planes,
    field, perm_hbm, turnx_hbm, xfirst_hbm, xlow_hbm, yhigh_hbm, ylow_hbm, turny_hbm,
    out,
    raw, s1, r1, s2, r2, s3, r3, zed, perm, turnx, xfirst, xlow, yhigh, ylow, turny,
    in_sem, tab_sem, ss1, rs1, ssf, rsf, ss2, rs2, ss3, rs3,
):
    me, my = lax.axis_index("gx"), lax.axis_index("gy")
    code = gray(me)
    rows, cols = raw.shape[1:]
    tiles, wide = rows // SUB, cols // LANES
    freqs = r3.shape[3]
    groups = turny.shape[0]
    per = yhigh.shape[0]
    half = gx // 2
    units = 2 * planes

    def toggles(value, weights):
        return [(1 - value // w % 2 * 2) * w for w in weights]

    flip_me = toggles(me, [1 << i for i in range(gx.bit_length() - 1)])

    def flipped(value, flips, mask):
        for i, f in enumerate(flips):
            if mask >> i & 1:
                value = value + f
        return value

    def piece(place):
        return code // (2 * place) * place + code % place

    def by_family(c, body):
        for f, place in enumerate(PLACES):

            @pl.when(lax.rem(c, FAMILIES) == f)
            def _(place=place):
                body(place)

    def peers(place):
        return [(k, ungray(k // place * (2 * place) + k % place)) for k in range(half)]

    def load(c):
        return pltpu.make_async_copy(field.at[c], raw.at[c], in_sem.at[c])

    pairs = [(perm_hbm.at[my], perm)]
    for f in range(FAMILIES):
        pairs.append((turnx_hbm.at[piece(PLACES[f]) * 2 // wide], turnx.at[f]))
    pairs += [
        (xfirst_hbm, xfirst),
        (xlow_hbm, xlow),
        (yhigh_hbm, yhigh),
        (ylow_hbm, ylow),
        (turny_hbm, turny),
    ]
    loads = [pltpu.make_async_copy(a, b, tab_sem.at[i]) for i, (a, b) in enumerate(pairs)]

    barrier = pltpu.get_barrier_semaphore()

    def greet(i, _):
        pl.semaphore_signal(barrier, inc=1, device_id=(lax.rem(me + i, gx), my), device_id_type=MESH)
        return 0

    lax.fori_loop(1, gx, greet, 0)
    for j in range(1, gy):
        pl.semaphore_signal(barrier, inc=1, device_id=(me, lax.rem(my + j, gy)), device_id_type=MESH)
    loads[0].start()
    lax.fori_loop(0, planes, lambda c, _: (load(c).start(), 0)[1], 0)
    for copy in loads[1:]:
        copy.start()
    pl.semaphore_wait(barrier, gx + gy - 2)
    loads[0].wait()

    def send(source, target, send_sem, recv_sem, device_id):
        pltpu.make_async_remote_copy(
            src_ref=source,
            dst_ref=target,
            send_sem=send_sem,
            recv_sem=recv_sem,
            device_id=device_id,
            device_id_type=MESH,
        ).start()

    def wait(ref, sem):
        pltpu.make_async_copy(ref, ref, sem).wait()

    def exchange_raw(c):
        def body(place):
            own = piece(place)
            flips = toggles(own, [1 << i for i in range(half.bit_length() - 1)])
            pltpu.make_async_copy(s1.at[c, own], r1.at[c, me], rs1.at[c]).start()
            for k, mask in peers(place)[1:]:
                there = (flipped(me, flip_me, mask), my)
                send(s1.at[c, flipped(own, flips, k)], r1.at[c, me], ss1, rs1.at[c], there)

        by_family(c, body)

    def forward(c):
        def body(place):
            other = (flipped(me, flip_me, ungray(place)), my)
            for k, mask in peers(place):
                g = flipped(me, flip_me, mask)
                send(r1.at[c, g], r1.at[c, g], ssf, rsf.at[c], other)

        by_family(c, body)

    def exchange_x(c):
        def body(place):
            own = piece(place)
            pltpu.make_async_copy(s2.at[c, me], r2.at[c, own], rs2.at[c]).start()
            for k, mask in peers(place)[1:]:
                there = flipped(me, flip_me, mask)
                send(s2.at[c, there], r2.at[c, own], ss2, rs2.at[c], (there, my))

        by_family(c, body)

    def exchange_y(c):
        pltpu.make_async_copy(s3.at[my, c], r3.at[my, c], rs3.at[c]).start()
        for j in range(1, gy):
            t = lax.rem(my + j, gy)
            send(s3.at[t, c], r3.at[my, c], ss3, rs3.at[c], (me, t))

    def permute(c):
        load(c).wait()
        high, low = split(raw[c])
        both = jnp.dot(jnp.concatenate([high, low], axis=0), perm[...], preferred_element_type=F32)
        moved = both[:rows] + both[rows:]
        for t in range(tiles):
            for w in range(wide):
                s1[2 * c + w % 2, (t * wide + w) // 2] = moved[t * SUB : (t + 1) * SUB, w * LANES : (w + 1) * LANES]

    def over_gx(c):
        family = lax.rem(c, FAMILIES)

        got = real_fft([r1[c, g] for g in range(gx)])
        for i in range(gx):
            r = bit_reverse(i, gx.bit_length() - 1)
            re, im = got[r] if 2 * r <= gx else conj(got[gx - r])
            if r == 0:
                s2[c, i, 0] = re
                s2[c, i, 1] = jnp.zeros_like(re)
                continue
            tr, ti = turnx[family, i, 0], turnx[family, i, 1]
            if im is None:
                s2[c, i, 0] = re * tr
                s2[c, i, 1] = re * ti
            else:
                s2[c, i, 0] = re * tr - im * ti
                s2[c, i, 1] = re * ti + im * tr

    def over_m(c):
        value = jnp.concatenate(
            [
                jnp.concatenate(
                    [r2[c, t * wide // 2 + w, part] for part in range(2) for t in range(tiles)], axis=0
                )
                for w in range(wide // 2)
            ],
            axis=1,
        )
        high, low = split(value)
        done = jnp.dot(xfirst[...], jnp.concatenate([high, low], axis=0), preferred_element_type=F32)
        done = done + jnp.dot(xlow[...], high, preferred_element_type=F32)
        for part in range(2):
            for s in range(gy):
                first = part * rows + s * freqs
                s3[s, c, part] = done[first : first + freqs]

    def over_y(c):
        group = lax.broadcasted_iota(jnp.int32, (freqs, LANES), 1) // (LANES // per)
        for q in range(per):
            lines = []
            for w in range(wide):
                halves = []
                for part in range(2):
                    at = slice(w // 2 * LANES, (w // 2 + 1) * LANES)
                    got = [r3[s, 2 * c + w % 2, part, :, at] for s in range(gy)]
                    merged = got[-q % per]
                    for g in range(1, per):
                        merged = jnp.where(group == g, got[(g - q) % per], merged)
                    halves.append(merged)
                lines.append(jnp.concatenate(halves, axis=1))
            high, low = split(jnp.concatenate(lines, axis=0))
            both = jnp.dot(jnp.concatenate([high, low], axis=0), yhigh[q], preferred_element_type=F32)
            total = wide * freqs
            done = both[:total] + both[total:] + jnp.dot(high, ylow[q], preferred_element_type=F32)
            for w in range(wide):
                zed[w * per + q] = done[w * freqs : (w + 1) * freqs]
        for b in range(freqs // SUB):
            at = slice(b * SUB, (b + 1) * SUB)
            values = []
            for e in range(groups):
                re, im = zed[e, at, :LANES], zed[e, at, LANES:]
                if e == 0:
                    values.append((re, im))
                else:
                    tr, ti = turny[e, 0], turny[e, 1]
                    values.append((re * tr - im * ti, re * ti + im * tr))
            for k, (re, im) in enumerate(complex_fft(values)):
                out[0, c, at, k * LANES : (k + 1) * LANES] = re
                out[1, c, at, k * LANES : (k + 1) * LANES] = im

    def enter(c, _):
        @pl.when(lax.rem(c, 2) == 0)
        def _():
            permute(lax.div(c, 2))

        exchange_raw(c)
        return 0

    lax.fori_loop(0, AHEAD, enter, 0)
    for copy in loads[1:]:
        copy.wait()

    def turn_step(i, _):
        @pl.when(i < units - AHEAD)
        def _():
            enter(i + AHEAD, 0)

        @pl.when(i < units)
        def _():
            wait(r1.at[i, pl.ds(0, half)], rs1.at[i])
            forward(i)

        @pl.when(jnp.logical_and(i >= LAG_A, i < units + LAG_A))
        def _():
            c = i - LAG_A
            wait(r1.at[c, pl.ds(0, half)], rsf.at[c])
            over_gx(c)
            exchange_x(c)

        @pl.when(jnp.logical_and(i >= LAG_B, i < units + LAG_B))
        def _():
            c = i - LAG_B
            wait(r2.at[c], rs2.at[c])
            over_m(c)
            exchange_y(c)

        @pl.when(i >= LAG_C)
        def _():
            c = i - LAG_C
            wait(r3.at[:, c], rs3.at[c])

            @pl.when(lax.rem(c, 2) == 1)
            def _():
                over_y(lax.div(c, 2))

        return 0

    lax.fori_loop(0, units + LAG_C, turn_step, 0)

    wait(s1.at[:, pl.ds(0, half - 1)], ss1)
    wait(r1.at[:, pl.ds(0, half)], ssf)
    wait(s2.at[:, pl.ds(0, half - 1)], ss2)
    wait(s3.at[pl.ds(0, gy - 1)], ss3)


def write_out(done, out, sems):
    size = done.shape[1] // (WRITES // 2)
    copies = []
    for i in range(WRITES):
        at = (i % 2, pl.ds(i // 2 * size, size))
        copies.append(pltpu.make_async_copy(done.at[at], out.at[at], sems.at[i]))
        copies[-1].start()
    for copy in copies:
        copy.wait()


def solution(mesh):
    gx, gy = mesh.shape["gx"], mesh.shape["gy"]

    def per_device(field):
        comp, depth, rows, cols = field.shape
        planes = comp * depth
        units = 2 * planes
        freqs = rows // gy
        ny = gy * cols
        groups = ny // LANES
        consts = tables(gx, gy, rows, cols, freqs)
        any_ = pl.BlockSpec(memory_space=pl.ANY)
        pieces = (rows // SUB) * (cols // LANES)
        assert pieces == gx
        vmem = lambda a: pltpu.VMEM(a.shape, a.dtype)
        dma = pltpu.SemaphoreType.DMA
        perm, turnx, xfirst, xlow, yhigh, ylow, turny = consts
        result = pl.pallas_call(
            functools.partial(kernel, gx, gy, planes),
            out_shape=pltpu.VMEM((2, planes, freqs, ny), F32),
            in_specs=[any_] * 8,
            out_specs=pl.BlockSpec(memory_space=pltpu.VMEM),
            scratch_shapes=[
                pltpu.VMEM((planes, rows, cols), F32),
                pltpu.VMEM((units, gx // 2, SUB, LANES), F32),
                pltpu.VMEM((units, gx, SUB, LANES), F32),
                pltpu.VMEM((units, gx, 2, SUB, LANES), F32),
                pltpu.VMEM((units, gx // 2, 2, SUB, LANES), F32),
                pltpu.VMEM((gy, units, 2, freqs, cols // 2), F32),
                pltpu.VMEM((gy, units, 2, freqs, cols // 2), F32),
                pltpu.VMEM((groups, freqs, 2 * LANES), F32),
                pltpu.VMEM(perm.shape[1:], perm.dtype),
                pltpu.VMEM((FAMILIES,) + turnx.shape[1:], turnx.dtype),
                vmem(xfirst),
                vmem(xlow),
                vmem(yhigh),
                vmem(ylow),
                vmem(turny),
                dma((planes,)),
                dma((6 + FAMILIES,)),
                *[pltpu.SemaphoreType.DMA, dma((units,))] * 4,
            ],
            compiler_params=pltpu.CompilerParams(
                collective_id=0, has_side_effects=True, vmem_limit_bytes=50 << 20
            ),
        )(field.reshape(planes, rows, cols), *[jnp.asarray(c) for c in consts])
        result = pltpu.with_memory_space_constraint(result, pltpu.VMEM)
        result = pl.pallas_call(
            write_out,
            out_shape=jax.ShapeDtypeStruct(result.shape, F32),
            in_specs=[pl.BlockSpec(memory_space=pltpu.VMEM)],
            out_specs=any_,
            scratch_shapes=[dma((WRITES,))],
            compiler_params=pltpu.CompilerParams(vmem_limit_bytes=8 << 20),
        )(result)
        return result.reshape(2, comp, depth, freqs, ny)

    return jax.shard_map(
        per_device,
        mesh=mesh,
        in_specs=(P(None, None, "gx", "gy"),),
        out_specs=P(None, None, None, ("gx", "gy"), None),
        check_vma=False,
    )
```
